256 devices in a mesh: row: 8 (over z_hi, core), col: 32 (over x, z_lo, y).
Axes of the slice: x: 4, y: 4, z: 8 (z_hi: 4, z_lo: 2; z = z_hi * 2 + z_lo), core: 2. Of those that a mesh axis runs over, the one named last changes fastest.
Arguments:
- grad_out: bfloat16 [98304, 512], P(('row', 'col')), may hold values from -6 to 6
- features: bfloat16 [98304, 512], P(('row', 'col')), may hold values from -0.01953125 to 0.01953125
- weight: bfloat16 [512, 512], replicated, may hold values from -0.25 to 0.25
- degrees: int32 [98304], P(('row', 'col')), may hold values from 1 to 16
- block_coords: int32 [8, 32, 160, 2], P('row', 'col'), may hold values from 0 to 95, as said below
- block_values: bfloat16 [8, 32, 160, 128, 128], P('row', 'col'), may hold values from -0.21875 to 0.21875
- block_counts: int32 [8, 32], P('row', 'col'), may hold values from 1 to 160, as said below
Outputs:
- grad_features: bfloat16 [98304, 512], P(('row', 'col'))
- grad_weight: float32 [512, 512], replicated
The draws below stay inside these ranges and needn't reach their ends.
Inputs may be any that keep to these rules, and one draw needn't show every extreme that they name: `block_counts`: each tile has 1 to 160 live slots, and some tile has exactly 160. `block_coords`: within a tile the 160 slots name distinct blocks; the first coordinate is below 24, the second below 96.
All inputs are finite; a program needn't handle non-finite values.
Results may differ from the reference program's by a relative error of at most 0.02.
Values may be sent and summed in bfloat16 or wider, within the bound.
A program may use at most 192 MiB of HBM per device.

```python
import jax
import jax.numpy as jnp
from jax import lax

F = 512
BLOCK = 128
SLAB = 384
CAP = 160
GRID_R = 8
GRID_C = 32
NODES = 98304
TILE_ROWS = 24
TILE_COLS = 96


def tile_positions(one_key):
    return jax.random.permutation(one_key, TILE_ROWS * TILE_COLS)[:CAP]


def draw_block_coords(key, part):
    key = jax.random.fold_in(key, 11)
    tile_keys = jax.random.split(key, GRID_R * GRID_C)
    positions = jax.vmap(tile_positions)(tile_keys)
    coords = jnp.stack([positions // TILE_COLS, positions % TILE_COLS], axis=-1).astype(jnp.int32)
    return coords.reshape(GRID_R, GRID_C, CAP, 2)


def draw_block_counts(key, part):
    key = jax.random.fold_in(key, 23)
    draw_key, pick_key = jax.random.split(key)
    counts = jax.random.randint(draw_key, (GRID_R * GRID_C,), 1, CAP + 1)
    chosen = jax.random.randint(pick_key, (), 0, GRID_R * GRID_C)
    counts = jnp.where(jnp.arange(GRID_R * GRID_C) == chosen, CAP, counts)
    return counts.reshape(GRID_R, GRID_C).astype(jnp.int32)


def set_ends(values, rng, low, top_value):
    longest = values.shape.index(max(values.shape))
    spots = []
    for shift in (0, 1):
        where = [jax.random.randint(jax.random.fold_in(rng, axis), (), 0, length) for axis, length in enumerate(values.shape)]
        where[longest] = (where[longest] + shift) % values.shape[longest]
        spots.append(tuple(where))
    return values.at[spots[0]].set(low).at[spots[1]].set(top_value)


def shard_levels(rng, shape, shards, smallest, high):
    factor_of, own = 1.0, jax.random.fold_in(rng, 6)
    for dim, blocks in shards:
        draws = jnp.exp(jax.random.uniform(jax.random.fold_in(own, dim), (blocks,), jnp.float32, smallest / len(shards), high / len(shards)))
        factor_of = factor_of * jnp.repeat(draws, shape[dim] // blocks).reshape([-1 if axis == dim else 1 for axis in range(len(shape))])
    return factor_of


def bell_draw(stream_key, extent, spread, most, cuts=(), kind=jnp.bfloat16):
    gain = shard_levels(stream_key, extent, cuts, -0.22, 0.18) if cuts else 1.0
    drawn = jax.random.normal(stream_key, extent, jnp.float32) * spread * gain
    return jnp.minimum(jnp.maximum(drawn, -most), most).astype(kind)


def setup_inputs(seed: int = 0) -> dict:
    splits = jax.random.split(jax.random.key(seed), 8)
    grad_out = bell_draw(splits[0], (NODES, F), 1.0, 6.0, ((0, 256),))
    features = bell_draw(splits[1], (NODES, F), NODES ** -0.5, 0.01953125, ((0, 256),))
    weight = bell_draw(splits[2], (F, F), F ** -0.5, 0.25)
    degrees = set_ends(jax.random.randint(splits[3], (NODES,), 1, 17), jax.random.fold_in(splits[3], 1), 1, 16).astype(jnp.int32)
    block_coords = draw_block_coords(jax.random.fold_in(splits[7], 71), 0)
    block_values = bell_draw(splits[5], (GRID_R, GRID_C, CAP, BLOCK, BLOCK), (CAP * BLOCK * BLOCK // (8 * SLAB)) ** -0.5, 0.21875, ((0, 8), (1, 32)))
    block_counts = draw_block_counts(jax.random.fold_in(splits[7], 71), 0)
    return dict(grad_out=grad_out, features=features, weight=weight, degrees=degrees, block_coords=block_coords, block_values=block_values, block_counts=block_counts)


def reference(grad_out, features, weight, degrees, block_coords, block_values, block_counts):
    per_slab = SLAB // BLOCK
    span_blocks = GRID_C * per_slab
    tile_count = GRID_R * GRID_C
    inv_root = lax.rsqrt(degrees.astype(jnp.float32))
    scaled = (grad_out.astype(jnp.float32) * inv_root[:, None]).astype(jnp.bfloat16)
    source = scaled.reshape(NODES // BLOCK, BLOCK, F)
    flat_coords = block_coords.reshape(tile_count, CAP, 2)
    flat_values = block_values.reshape(tile_count, CAP, BLOCK, BLOCK)
    flat_counts = block_counts.reshape(tile_count)
    tile_ids = jnp.arange(tile_count, dtype=jnp.int32)

    def one_tile(aggregate, inputs):
        tile_id, tile_coords, tile_values, live_count = inputs
        grid_row = tile_id // GRID_C
        grid_col = tile_id % GRID_C
        row_block = tile_coords[:, 0]
        global_rows = ((row_block // per_slab * GRID_C + grid_col) * per_slab + row_block % per_slab).astype(jnp.int32)
        picked = source[global_rows].astype(jnp.float32)
        contribution = jnp.einsum('sab,saf->sbf', tile_values.astype(jnp.float32), picked)
        slot_live = jnp.arange(CAP, dtype=jnp.int32) < live_count
        contribution = jnp.where(slot_live[:, None, None], contribution, jnp.float32(0.0))
        partial_value = jnp.zeros((span_blocks, BLOCK, F), jnp.float32).at[tile_coords[:, 1]].add(contribution)
        partial_value = lax.optimization_barrier(partial_value.astype(jnp.bfloat16)).astype(jnp.float32)
        start = (grid_row * span_blocks).astype(jnp.int32)
        current = lax.dynamic_slice_in_dim(aggregate, start, span_blocks, 0)
        aggregate = lax.dynamic_update_slice_in_dim(aggregate, current + partial_value, start, 0)
        return (aggregate, tile_id)
    aggregate = jnp.zeros((NODES // BLOCK, BLOCK, F), jnp.float32)
    aggregate, visited = lax.scan(one_tile, aggregate, (tile_ids, flat_coords, flat_values, flat_counts))
    grad_agg = (aggregate.reshape(NODES, F) * inv_root[:, None]).astype(jnp.bfloat16)
    grad_features = lax.dot_general(grad_agg, weight, (((1,), (1,)), ((), ())), preferred_element_type=jnp.float32).astype(jnp.bfloat16)
    grad_weight = lax.dot_general(features, grad_agg, (((0,), (0,)), ((), ())), preferred_element_type=jnp.float32)
    return (grad_features, grad_weight)
```

```python
import functools

import jax
import jax.numpy as jnp
from jax import lax
from jax.experimental import pallas as pl
from jax.experimental.pallas import tpu as pltpu
from jax.sharding import PartitionSpec as P

MESH = pl.DeviceIdType.MESH
F32, BF16 = jnp.float32, jnp.bfloat16
CAP = 160
EDGE = 128
COLS = 96
PER = 3
PARTS = 4


def fused(
    meta, values_hbm, source_hbm, scale, features, weight,
    out_features, out_weight,
    values, source, run, part, ring1, ring2, mid, ring3, ring4, last_sum, z_in, agg,
    w_send, w_own, w_in, w_plane, w_piece, w_line, w_z, w_full, w_sib,
    load_sem, ring_send, ring_recv, z_send, z_recv, sib_send, sib_recv,
    plane_send, plane_recv, line_send, line_recv,
):
    row, col = lax.axis_index("row"), lax.axis_index("col")
    core = lax.rem(row, 2)
    z_hi = row // 2
    x, z_lo, y = col // 8, lax.rem(col // 4, 2), lax.rem(col, 4)
    z = z_hi * 2 + z_lo
    plane = x * 4 + y

    def at(ix=x, iz=z, iy=y, icore=core):
        return ((iz // 2) * 2 + icore, (ix * 2 + lax.rem(iz, 2)) * 4 + iy)

    def plane_dev(p):
        return at(ix=p // 4, iy=lax.rem(p, 4))

    sibling = at(icore=1 - core)

    load_v = pltpu.make_async_copy(values_hbm, values, load_sem.at[0])
    load_s = pltpu.make_async_copy(source_hbm, source, load_sem.at[1])
    load_v.start()
    load_s.start()

    barrier = pltpu.get_barrier_semaphore()

    def greet_plane(i, carry):
        pl.semaphore_signal(barrier, inc=1, device_id=plane_dev(lax.rem(plane + i, 16)), device_id_type=MESH)
        return carry

    def greet_line(i, carry):
        pl.semaphore_signal(barrier, inc=1, device_id=at(iz=lax.rem(z + i, 8)), device_id_type=MESH)
        return carry

    lax.fori_loop(1, 16, greet_plane, 0)
    lax.fori_loop(1, 8, greet_line, 0)
    pl.semaphore_signal(barrier, inc=1, device_id=sibling, device_id_type=MESH)
    load_v.wait()
    load_s.wait()
    pl.semaphore_wait(barrier, 23)

    def products(pair):
        lanes = slice(pair * 256, pair * 256 + 256)

        def slot(t, acc):
            block = values[meta[t]]
            rows = source[meta[CAP + t], :, lanes]
            prod = lax.dot_general(block, rows, (((0,), (0,)), ((), ())), preferred_element_type=F32)
            acc = jnp.where(meta[2 * CAP + t] == 1, prod, acc + prod)
            run[t] = acc.astype(BF16)
            return acc

        lax.fori_loop(0, CAP, slot, jnp.zeros((EDGE, 256), F32), unroll=4)

        def place(i, carry):
            u, v, zz, p = i // 24, lax.rem(i // 6, 4), lax.rem(i // 3, 2), lax.rem(i, 3)
            for side in (0, 1):
                b = (((u * 2 + zz) * 4 + v) if side == 0 else ((v * 2 + zz) * 4 + u)) * PER + p
                end = meta[3 * CAP + b]
                got = run[jnp.maximum(end, 0), :, side * 128:side * 128 + 128]
                part[pair * 2 + side, i] = jnp.where(end >= 0, got, jnp.zeros_like(got))
            return carry

        lax.fori_loop(0, COLS, place, 0, unroll=2)

    def ring(j, stage):
        side = (j + stage) % 2
        u = x if side == 0 else y
        n = 24 if stage == 0 else 6
        h = n // 2
        src = part.at[j] if stage == 0 else mid.at[j]
        one = ring1.at[j] if stage == 0 else ring3.at[j]
        two = ring2.at[j] if stage == 0 else ring4.at[j]
        right, left, far = lax.rem(u + 1, 4), lax.rem(u + 3, 4), lax.rem(u + 2, 4)
        dev = (lambda k: at(ix=k)) if side == 0 else (lambda k: at(iy=k))

        def copy(k, a, b, to):
            return pltpu.make_async_remote_copy(
                src_ref=a, dst_ref=b, send_sem=ring_send.at[j, stage, k], recv_sem=ring_recv.at[j, stage, k],
                device_id=dev(to), device_id_type=MESH,
            )

        c = [
            copy(0, src.at[pl.ds(far * n, h)], one.at[0], right),
            copy(1, src.at[pl.ds(far * n + h, h)], one.at[1], left),
            copy(2, src.at[pl.ds(right * n + h, h)], two.at[0, pl.ds(h, h)], right),
            copy(3, src.at[pl.ds(left * n, h)], two.at[1, pl.ds(0, h)], left),
            copy(4, one.at[0], two.at[0, pl.ds(0, h)], right),
            copy(5, one.at[1], two.at[1, pl.ds(h, h)], left),
        ]

        def first():
            for k in range(4):
                c[k].start()

        def second():
            for k, base in ((0, right * n), (1, left * n + h)):
                c[k].wait_recv()

                def add(i, carry):
                    one[k, i] = (one[k, i].astype(F32) + src[base + i].astype(F32)).astype(BF16)
                    return carry

                lax.fori_loop(0, h, add, 0)
                c[4 + k].start()

        def third(write):
            for k in range(2, 6):
                c[k].wait_recv()

            def add(i, carry):
                write(i, src[u * n + i].astype(F32) + two[0, i].astype(F32) + two[1, i].astype(F32))
                return carry

            lax.fori_loop(0, n, add, 0)

        def drain():
            for k in range(6):
                c[k].wait_send()

        return first, second, third, drain

    rings = {(j, s): ring(j, s) for j in range(PARTS) for s in (0, 1)}
    z_copy = [
        pltpu.make_async_remote_copy(
            src_ref=last_sum.at[j, pl.ds((1 - z_lo) * PER, PER)], dst_ref=z_in.at[j],
            send_sem=z_send.at[j], recv_sem=z_recv.at[j],
            device_id=at(iz=z_hi * 2 + 1 - z_lo), device_id_type=MESH,
        )
        for j in range(PARTS)
    ]

    for pair in (0, 1):
        products(pair)
        rings[2 * pair, 0][0]()
        rings[2 * pair + 1, 0][0]()
    for j in range(PARTS):
        rings[j, 0][1]()
    for j in range(PARTS):
        def to_mid(i, v, j=j):
            mid[j, i] = v.astype(BF16)
        rings[j, 0][2](to_mid)
        rings[j, 1][0]()
    for j in range(PARTS):
        rings[j, 1][1]()
    for j in range(PARTS):
        def to_last(i, v, j=j):
            last_sum[j, i] = v.astype(BF16)
        rings[j, 1][2](to_last)
        z_copy[j].start()
    for j in range(PARTS):
        z_copy[j].wait_recv()
        for p in range(PER):
            total = last_sum[j, z_lo * PER + p].astype(F32) + z_in[j, p].astype(F32)
            agg[p * 128:p * 128 + 128, j * 128:j * 128 + 128] = (total * scale[p * 128:p * 128 + 128, :]).astype(BF16)

    def weight_half(which, dst):
        f = features[:, pl.ds(pl.multiple_of(which * 256, 256), 256)]
        for j in range(PARTS):
            d = lax.dot_general(f, agg[:, j * 128:j * 128 + 128], (((0,), (0,)), ((), ())), preferred_element_type=F32)
            for q in range(4):
                dst[j * 4 + q] = d[q * 64:q * 64 + 64, :]

    def remote(src, dst, ss, rs, to):
        return pltpu.make_async_remote_copy(
            src_ref=src, dst_ref=dst, send_sem=ss, recv_sem=rs, device_id=to, device_id_type=MESH
        )

    weight_half(1 - core, w_send)
    give = remote(w_send, w_in, sib_send.at[0], sib_recv.at[0], sibling)
    give.start()
    weight_half(core, w_own)
    give.wait_recv()
    for p in range(16):
        w_own[p] = w_own[p] + w_in[p]

    def all_to_all(count, me, dev, copy_of):
        def go(i, carry):
            to = lax.rem(me + i, count)
            copy_of(to, me, dev(to)).start()
            return carry

        def arrive(i, carry):
            frm = lax.rem(me + i, count)
            copy_of(me, frm, dev(frm)).wait_recv()
            return carry

        def drain(i, carry):
            to = lax.rem(me + i, count)
            copy_of(to, me, dev(to)).wait_send()
            return carry

        return (
            lambda: lax.fori_loop(1, count, go, 0),
            lambda: lax.fori_loop(1, count, arrive, 0),
            lambda: lax.fori_loop(1, count, drain, 0),
        )

    def line_dev(k):
        return at(iz=k)

    plane_go, plane_arrive, plane_drain = all_to_all(16, plane, plane_dev, lambda to, frm, d: remote(
        w_own.at[to], w_plane.at[frm], plane_send.at[0, to], plane_recv.at[0, frm], d))
    line_go, line_arrive, line_drain = all_to_all(8, z, line_dev, lambda to, frm, d: remote(
        w_piece.at[to], w_line.at[frm], line_send.at[0, to], line_recv.at[0, frm], d))
    line_go2, line_arrive2, line_drain2 = all_to_all(8, z, line_dev, lambda to, frm, d: remote(
        w_z.at[z], w_z.at[frm], line_send.at[1, to], line_recv.at[1, frm], d))
    plane_go2, plane_arrive2, plane_drain2 = all_to_all(16, plane, plane_dev, lambda to, frm, d: remote(
        w_full.at[plane], w_full.at[frm], plane_send.at[1, to], plane_recv.at[1, frm], d))

    plane_go()
    out_features[...] = lax.dot_general(
        agg[...], weight[...], (((1,), (1,)), ((), ())), preferred_element_type=F32
    ).astype(BF16)
    w_plane[plane] = w_own[plane]
    plane_arrive()
    total = w_plane[0]
    for p in range(1, 16):
        total = total + w_plane[p]
    for k in range(8):
        w_piece[k] = total[k * 8:k * 8 + 8, :]
    line_go()
    w_line[z] = w_piece[z]
    line_arrive()
    total = w_line[0]
    for k in range(1, 8):
        total = total + w_line[k]
    w_z[z] = total
    line_go2()
    line_arrive2()
    for k in range(8):
        w_full[plane, k * 8:k * 8 + 8, :] = w_z[k]
    plane_go2()
    plane_arrive2()
    back = remote(w_full, w_sib, sib_send.at[1], sib_recv.at[1], sibling)
    back.start()
    mine = pl.multiple_of(core * 256, 256)
    other = pl.multiple_of((1 - core) * 256, 256)
    for j in range(PARTS):
        for q in range(4):
            out_weight[pl.ds(mine + q * 64, 64), j * 128:j * 128 + 128] = w_full[j * 4 + q]
    back.wait_recv()
    for j in range(PARTS):
        for q in range(4):
            out_weight[pl.ds(other + q * 64, 64), j * 128:j * 128 + 128] = w_sib[j * 4 + q]

    for key in rings:
        rings[key][3]()
    for j in range(PARTS):
        z_copy[j].wait_send()
    give.wait_send()
    back.wait_send()
    plane_drain()
    line_drain()
    line_drain2()
    plane_drain2()


def slot_table(coords, count):
    index = jnp.arange(CAP, dtype=jnp.int32)
    live = index < count
    rows, cols = coords[:, 0], coords[:, 1]
    key = jnp.where(live, cols * 32 + rows, 4096 + index)
    rank = jnp.sum((key[None, :] < key[:, None]).astype(jnp.int32), axis=1)
    hit = rank[None, :] == index[:, None]
    pick = lambda v: jnp.sum(jnp.where(hit, v[None, :], 0), axis=1)
    first = jnp.ones((CAP,), jnp.int32)
    order, srow, scol = pick(index), pick(rows), pick(cols)
    first = jnp.concatenate([first[:1], (scol[1:] != scol[:-1]).astype(jnp.int32)])
    lanes = jnp.arange(COLS, dtype=jnp.int32)[:, None]
    upto = jnp.sum((live & (cols <= lanes)).astype(jnp.int32), axis=1)
    has = jnp.any(live & (cols == lanes), axis=1)
    end = jnp.where(has, upto - 1, -1)
    return jnp.concatenate([order, srow, first, end, jnp.zeros((CAP - COLS,), jnp.int32)])


def body(grad_out, features, weight, degrees, block_coords, block_values, block_counts):
    inv_root = lax.rsqrt(degrees.astype(F32))
    scaled = (grad_out.astype(F32) * inv_root[:, None]).astype(BF16)
    gathered = lax.all_gather(scaled, "row", axis=0, tiled=True).reshape(24, EDGE, 512)
    meta = slot_table(block_coords[0, 0], block_counts[0, 0])
    scale = jnp.broadcast_to(inv_root[:, None], (384, 128))
    vm = lambda *s: pltpu.VMEM(s, BF16)
    vf = lambda *s: pltpu.VMEM(s, F32)
    dma = lambda *s: pltpu.SemaphoreType.DMA(s)
    any_spec, vmem_spec = pl.BlockSpec(memory_space=pl.ANY), pl.BlockSpec(memory_space=pltpu.VMEM)
    return pl.pallas_call(
        fused,
        out_shape=(jax.ShapeDtypeStruct((384, 512), BF16), jax.ShapeDtypeStruct((512, 512), F32)),
        in_specs=[pl.BlockSpec(memory_space=pltpu.SMEM), any_spec, any_spec, vmem_spec, vmem_spec, vmem_spec],
        out_specs=(vmem_spec, vmem_spec),
        scratch_shapes=[
            vm(CAP, EDGE, EDGE), vm(24, EDGE, 512), vm(CAP, EDGE, 256), vm(PARTS, COLS, EDGE, EDGE),
            vm(PARTS, 2, 12, EDGE, EDGE), vm(PARTS, 2, 24, EDGE, EDGE), vm(PARTS, 24, EDGE, EDGE),
            vm(PARTS, 2, 3, EDGE, EDGE), vm(PARTS, 2, 6, EDGE, EDGE), vm(PARTS, 6, EDGE, EDGE),
            vm(PARTS, PER, EDGE, EDGE), vm(384, 512),
            vf(16, 64, 128), vf(16, 64, 128), vf(16, 64, 128), vf(16, 64, 128), vf(8, 8, 128), vf(8, 8, 128),
            vf(8, 8, 128), vf(16, 64, 128), vf(16, 64, 128),
            dma(2), dma(PARTS, 2, 6), dma(PARTS, 2, 6), dma(PARTS), dma(PARTS), dma(2), dma(2),
            dma(2, 16), dma(2, 16), dma(2, 8), dma(2, 8),
        ],
        compiler_params=pltpu.CompilerParams(
            collective_id=0, has_side_effects=True, vmem_limit_bytes=60 * 1024 * 1024
        ),
    )(meta, block_values[0, 0], gathered, scale, features, weight)


def solution(mesh):
    in_specs = (
        P(("row", "col"), None),
        P(("row", "col"), None),
        P(),
        P(("row", "col")),
        P("row", "col", None, None),
        P("row", "col", None, None, None),
        P("row", "col"),
    )
    out_specs = (P(("row", "col"), None), P())
    return jax.shard_map(body, mesh=mesh, in_specs=in_specs, out_specs=out_specs, check_vma=False)
```

```python
import functools

import jax
import jax.numpy as jnp
from jax import lax
from jax.experimental import pallas as pl
from jax.experimental.pallas import tpu as pltpu
from jax.sharding import PartitionSpec as P

MESH = pl.DeviceIdType.MESH
F32, BF16 = jnp.float32, jnp.bfloat16
CAP = 160
EDGE = 128
COLS = 96
PER = 3
PARTS = 4
UNROLL = 16


def fused(
    meta, values_hbm, grad_out, scale, features, weight,
    out_features, out_weight,
    values, source0, source1, source2, source3, run, part, ring1, ring2, mid, ring3, ring4, last_sum, z_in, agg,
    w_send, w_own, w_in, w_out, w_plane, w_line, w_full, w_sib,
    load_sem, get_send, get_recv, ring_send, ring_recv, z_send, z_recv, sib_send, sib_recv,
    plane_send, plane_recv, line_send, line_recv,
):
    row, col = lax.axis_index("row"), lax.axis_index("col")
    core = lax.rem(row, 2)
    z_hi = row // 2
    x, z_lo, y = col // 8, lax.rem(col // 4, 2), lax.rem(col, 4)
    z = z_hi * 2 + z_lo
    plane = x * 4 + y

    def at(ix=x, iz=z, iy=y, icore=core):
        return ((iz // 2) * 2 + icore, (ix * 2 + lax.rem(iz, 2)) * 4 + iy)

    def plane_dev(p):
        return at(ix=p // 4, iy=lax.rem(p, 4))

    def line_dev(k):
        return at(iz=k)

    def remote(src, dst, ss, rs, to):
        return pltpu.make_async_remote_copy(
            src_ref=src, dst_ref=dst, send_sem=ss, recv_sem=rs, device_id=to, device_id_type=MESH
        )

    sibling = at(icore=1 - core)
    source = (source0, source1, source2, source3)

    load_v = pltpu.make_async_copy(values_hbm, values, load_sem)
    load_v.start()

    barrier = pltpu.get_barrier_semaphore()

    def greet_plane(i, carry):
        pl.semaphore_signal(barrier, inc=1, device_id=plane_dev(lax.rem(plane + i, 16)), device_id_type=MESH)
        return carry

    def greet_line(i, carry):
        pl.semaphore_signal(barrier, inc=1, device_id=line_dev(lax.rem(z + i, 8)), device_id_type=MESH)
        return carry

    lax.fori_loop(1, 16, greet_plane, 0)
    lax.fori_loop(1, 8, greet_line, 0)
    pl.semaphore_signal(barrier, inc=1, device_id=sibling, device_id_type=MESH)

    for j in range(PARTS):
        for p in range(PER):
            got = grad_out[p * 128:p * 128 + 128, j * 128:j * 128 + 128].astype(F32)
            source[j][row * PER + p] = (got * scale[p * 128:p * 128 + 128, :]).astype(BF16)

    pl.semaphore_wait(barrier, 23)

    def gather(j):
        up, down, far = lax.rem(z_hi + 1, 4), lax.rem(z_hi + 3, 4), lax.rem(z_hi + 2, 4)
        dev = lambda h: (h * 2 + core, col)
        cut = 1 + j % 2

        def copy(k, zh, to, start=0, size=PER):
            ref = source[j].at[pl.ds((zh * 2 + core) * PER + start, size)]
            return remote(ref, ref, get_send.at[j, k], get_recv.at[j, k], to)

        own_up, own_down, own_sib = copy(0, z_hi, dev(up)), copy(1, z_hi, dev(down)), copy(2, z_hi, sibling)
        fwd_up = copy(3, down, dev(up), 0, cut)
        fwd_down = copy(4, up, dev(down), cut, PER - cut)
        sib_down, sib_up = copy(5, down, sibling), copy(6, up, sibling)
        sib_far = copy(7, far, sibling)

        def own():
            own_up.start()
            own_down.start()
            own_sib.start()

        def forward():
            own_up.wait_recv()
            fwd_up.start()
            own_down.wait_recv()
            fwd_down.start()
            sib_down.start()
            sib_up.start()

        def finish():
            fwd_up.wait_recv()
            fwd_down.wait_recv()
            sib_far.start()
            own_sib.wait_recv()
            sib_down.wait_recv()
            sib_up.wait_recv()
            sib_far.wait_recv()

        def drain():
            for c in (own_up, own_down, own_sib, fwd_up, fwd_down, sib_down, sib_up, sib_far):
                c.wait_send()

        return own, forward, finish, drain

    gathers = [gather(j) for j in range(PARTS)]

    def products(j):
        def slot(t, acc):
            prod = lax.dot_general(
                values[meta[t]], source[j][meta[CAP + t]], (((0,), (0,)), ((), ())), preferred_element_type=F32
            )
            acc = jnp.where(meta[2 * CAP + t] == 1, prod, acc + prod)
            run[t] = acc.astype(BF16)
            return acc

        lax.fori_loop(0, CAP, slot, jnp.zeros((EDGE, EDGE), F32), unroll=UNROLL)

        def place(i, carry):
            u, v, zz, p = i // 24, lax.rem(i // 6, 4), lax.rem(i // 3, 2), lax.rem(i, 3)
            b = (((u * 2 + zz) * 4 + v) if j % 2 == 0 else ((v * 2 + zz) * 4 + u)) * PER + p
            end = meta[3 * CAP + b]
            got = run[jnp.maximum(end, 0)]
            part[j, i] = jnp.where(end >= 0, got, jnp.zeros_like(got))
            return carry

        lax.fori_loop(0, COLS, place, 0, unroll=4)

    def ring(j, stage):
        side = (j + stage) % 2
        u = x if side == 0 else y
        n = 24 if stage == 0 else 6
        h = n // 2
        src = part.at[j] if stage == 0 else mid.at[j]
        one = ring1.at[j] if stage == 0 else ring3.at[j]
        two = ring2.at[j] if stage == 0 else ring4.at[j]
        right, left, far = lax.rem(u + 1, 4), lax.rem(u + 3, 4), lax.rem(u + 2, 4)
        dev = (lambda k: at(ix=k)) if side == 0 else (lambda k: at(iy=k))

        def copy(k, a, b, to):
            return remote(a, b, ring_send.at[j, stage, k], ring_recv.at[j, stage, k], dev(to))

        c = [
            copy(0, src.at[pl.ds(far * n, h)], one.at[0], right),
            copy(1, src.at[pl.ds(far * n + h, h)], one.at[1], left),
            copy(2, src.at[pl.ds(right * n + h, h)], two.at[0, pl.ds(h, h)], right),
            copy(3, src.at[pl.ds(left * n, h)], two.at[1, pl.ds(0, h)], left),
            copy(4, one.at[0], two.at[0, pl.ds(0, h)], right),
            copy(5, one.at[1], two.at[1, pl.ds(h, h)], left),
        ]

        def first():
            for k in range(4):
                c[k].start()

        def second():
            for k, base in ((0, right * n), (1, left * n + h)):
                c[k].wait_recv()

                def add(i, carry):
                    one[k, i] = (one[k, i].astype(F32) + src[base + i].astype(F32)).astype(BF16)
                    return carry

                lax.fori_loop(0, h, add, 0)
                c[4 + k].start()

        def third():
            for k in range(2, 6):
                c[k].wait_recv()
            dst = mid if stage == 0 else last_sum

            def add(i, carry):
                v = src[u * n + i].astype(F32) + two[0, i].astype(F32) + two[1, i].astype(F32)
                dst[j, i] = v.astype(BF16)
                return carry

            lax.fori_loop(0, n, add, 0)

        def drain():
            for k in range(6):
                c[k].wait_send()

        return first, second, third, drain

    rings = {(j, s): ring(j, s) for j in range(PARTS) for s in (0, 1)}
    z_copy = [
        remote(
            last_sum.at[j, pl.ds((1 - z_lo) * PER, PER)], z_in.at[j], z_send.at[j], z_recv.at[j],
            at(iz=z_hi * 2 + 1 - z_lo),
        )
        for j in range(PARTS)
    ]

    def r1(j):
        rings[j, 0][0]()

    def r2(j):
        rings[j, 0][1]()

    def r3(j):
        rings[j, 0][2]()
        rings[j, 1][0]()

    def r4(j):
        rings[j, 1][1]()

    def r5(j):
        rings[j, 1][2]()
        z_copy[j].start()

    def r6(j):
        z_copy[j].wait_recv()
        for p in range(PER):
            total = last_sum[j, z_lo * PER + p].astype(F32) + z_in[j, p].astype(F32)
            agg[p * 128:p * 128 + 128, j * 128:j * 128 + 128] = (total * scale[p * 128:p * 128 + 128, :]).astype(BF16)

    def all_to_all(count, me, dev, copy_of):
        def go(i, carry):
            to = lax.rem(me + i, count)
            copy_of(to, me, dev(to)).start()
            return carry

        def arrive(i, carry):
            frm = lax.rem(me + i, count)
            copy_of(me, frm, dev(frm)).wait_recv()
            return carry

        def drain(i, carry):
            to = lax.rem(me + i, count)
            copy_of(to, me, dev(to)).wait_send()
            return carry

        return (
            lambda: lax.fori_loop(1, count, go, 0),
            lambda: lax.fori_loop(1, count, arrive, 0),
            lambda: lax.fori_loop(1, count, drain, 0),
        )

    def weight_sum(g):
        give = remote(w_send.at[g], w_in.at[g], sib_send.at[g, 0], sib_recv.at[g, 0], sibling)
        back = remote(w_full.at[g], w_sib.at[g], sib_send.at[g, 1], sib_recv.at[g, 1], sibling)
        go1, arrive1, drain1 = all_to_all(16, plane, plane_dev, lambda to, frm, d: remote(
            w_out.at[g, to], w_plane.at[g, frm], plane_send.at[g, 0, to], plane_recv.at[g, 0, frm], d))
        go2, arrive2, drain2 = all_to_all(8, z, line_dev, lambda to, frm, d: remote(
            w_line.at[g, z], w_line.at[g, frm], line_send.at[g, to], line_recv.at[g, frm], d))
        go3, arrive3, drain3 = all_to_all(16, plane, plane_dev, lambda to, frm, d: remote(
            w_full.at[g, plane], w_full.at[g, frm], plane_send.at[g, 1, to], plane_recv.at[g, 1, frm], d))

        def half(which, dst):
            f = features[:, pl.ds(pl.multiple_of(which * 256, 256), 256)]
            for k in range(2):
                lanes = slice((g * 2 + k) * 128, (g * 2 + k) * 128 + 128)
                d = lax.dot_general(f, agg[:, lanes], (((0,), (0,)), ((), ())), preferred_element_type=F32)
                for q in range(8):
                    dst[g, k * 8 + q] = d[q * 32:q * 32 + 32, :].astype(dst.dtype)

        def a():
            half(1 - core, w_send)
            give.start()
            half(core, w_own)

        def b():
            give.wait_recv()
            for p in range(16):
                w_out[g, p] = (w_own[g, p] + w_in[g, p].astype(F32)).astype(BF16)
            go1()
            w_plane[g, plane] = w_out[g, plane]

        def c():
            arrive1()
            total = w_plane[g, 0].astype(F32)
            for p in range(1, 16):
                total = total + w_plane[g, p].astype(F32)
            w_line[g, z] = total.astype(BF16)
            go2()

        def d():
            arrive2()
            total = w_line[g, 0].astype(F32)
            for k in range(1, 8):
                total = total + w_line[g, k].astype(F32)
            w_full[g, plane] = total.astype(BF16)
            go3()

        def write(which, src):
            base = pl.multiple_of(which * 256, 256)
            for k in range(2):
                for q in range(8):
                    out_weight[pl.ds(base + q * 32, 32), (g * 2 + k) * 128:(g * 2 + k) * 128 + 128] = (
                        src[g, k * 8 + q].astype(F32)
                    )

        def e():
            arrive3()
            back.start()
            write(core, w_full)

        def f():
            back.wait_recv()
            write(1 - core, w_sib)

        def drain():
            give.wait_send()
            back.wait_send()
            drain1()
            drain2()
            drain3()

        return a, b, c, d, e, f, drain

    ws = [weight_sum(g) for g in range(2)]

    gathers[0][0]()
    gathers[1][0]()
    gathers[0][1]()
    gathers[2][0]()
    gathers[0][2]()
    load_v.wait()
    for j in range(PARTS):
        if j + 1 < PARTS:
            gathers[j + 1][1]()
        if j + 3 < PARTS:
            gathers[j + 3][0]()
        products(j)
        r1(j)
        if j + 1 < PARTS:
            gathers[j + 1][2]()
        if j >= 2:
            r2(j - 2)
    r2(2)
    r3(0)
    r2(3)
    r3(1)
    r4(0)
    r3(2)
    r4(1)
    r3(3)
    r5(0)
    r5(1)
    r4(2)
    r4(3)
    r6(0)
    r6(1)
    ws[0][0]()
    r5(2)
    ws[0][1]()
    r5(3)
    ws[0][2]()
    r6(2)
    r6(3)
    ws[1][0]()
    ws[0][3]()
    ws[1][1]()
    out_features[...] = lax.dot_general(
        agg[...], weight[...], (((1,), (1,)), ((), ())), preferred_element_type=F32
    ).astype(BF16)
    ws[0][4]()
    ws[1][2]()
    ws[0][5]()
    ws[1][3]()
    ws[1][4]()
    ws[1][5]()

    for j in range(PARTS):
        gathers[j][3]()
    for key in rings:
        rings[key][3]()
    for j in range(PARTS):
        z_copy[j].wait_send()
    for g in range(2):
        ws[g][6]()


def slot_table(coords, count):
    index = jnp.arange(CAP, dtype=jnp.int32)
    live = index < count
    rows, cols = coords[:, 0], coords[:, 1]
    key = jnp.where(live, cols * 32 + rows, 4096 + index)
    rank = jnp.sum((key[None, :] < key[:, None]).astype(jnp.int32), axis=1)
    hit = rank[None, :] == index[:, None]
    pick = lambda v: jnp.sum(jnp.where(hit, v[None, :], 0), axis=1)
    first = jnp.ones((CAP,), jnp.int32)
    order, srow, scol = pick(index), pick(rows), pick(cols)
    first = jnp.concatenate([first[:1], (scol[1:] != scol[:-1]).astype(jnp.int32)])
    lanes = jnp.arange(COLS, dtype=jnp.int32)[:, None]
    upto = jnp.sum((live & (cols <= lanes)).astype(jnp.int32), axis=1)
    has = jnp.any(live & (cols == lanes), axis=1)
    end = jnp.where(has, upto - 1, -1)
    return jnp.concatenate([order, srow, first, end, jnp.zeros((CAP - COLS,), jnp.int32)])


def body(grad_out, features, weight, degrees, block_coords, block_values, block_counts):
    meta = slot_table(block_coords[0, 0], block_counts[0, 0])
    scale = lax.rsqrt(jnp.broadcast_to(degrees[:, None], (384, 128)).astype(F32))
    vm = lambda *s: pltpu.VMEM(s, BF16)
    vf = lambda *s: pltpu.VMEM(s, F32)
    dma = lambda *s: pltpu.SemaphoreType.DMA(s)
    any_spec, vmem_spec = pl.BlockSpec(memory_space=pl.ANY), pl.BlockSpec(memory_space=pltpu.VMEM)
    return pl.pallas_call(
        fused,
        out_shape=(jax.ShapeDtypeStruct((384, 512), BF16), jax.ShapeDtypeStruct((512, 512), F32)),
        in_specs=[pl.BlockSpec(memory_space=pltpu.SMEM), any_spec, vmem_spec, vmem_spec, vmem_spec, vmem_spec],
        out_specs=(vmem_spec, vmem_spec),
        scratch_shapes=[
            vm(CAP, EDGE, EDGE), vm(24, EDGE, EDGE), vm(24, EDGE, EDGE), vm(24, EDGE, EDGE), vm(24, EDGE, EDGE), vm(CAP, EDGE, EDGE), vm(PARTS, COLS, EDGE, EDGE),
            vm(PARTS, 2, 12, EDGE, EDGE), vm(PARTS, 2, 24, EDGE, EDGE), vm(PARTS, 24, EDGE, EDGE),
            vm(PARTS, 2, 3, EDGE, EDGE), vm(PARTS, 2, 6, EDGE, EDGE), vm(PARTS, 6, EDGE, EDGE),
            vm(PARTS, PER, EDGE, EDGE), vm(384, 512),
            vm(2, 16, 32, 128), vf(2, 16, 32, 128), vm(2, 16, 32, 128), vm(2, 16, 32, 128), vm(2, 16, 32, 128),
            vm(2, 8, 32, 128), vm(2, 16, 32, 128), vm(2, 16, 32, 128),
            pltpu.SemaphoreType.DMA, dma(PARTS, 8), dma(PARTS, 8), dma(PARTS, 2, 6), dma(PARTS, 2, 6),
            dma(PARTS), dma(PARTS), dma(2, 2), dma(2, 2),
            dma(2, 2, 16), dma(2, 2, 16), dma(2, 8), dma(2, 8),
        ],
        compiler_params=pltpu.CompilerParams(
            collective_id=0, has_side_effects=True, vmem_limit_bytes=60 * 1024 * 1024
        ),
    )(meta, block_values[0, 0], grad_out, scale, features, weight)


def solution(mesh):
    in_specs = (
        P(("row", "col"), None),
        P(("row", "col"), None),
        P(),
        P(("row", "col")),
        P("row", "col", None, None),
        P("row", "col", None, None, None),
        P("row", "col"),
    )
    out_specs = (P(("row", "col"), None), P())
    return jax.shard_map(body, mesh=mesh, in_specs=in_specs, out_specs=out_specs, check_vma=False)
```

```python
import functools

import jax
import jax.numpy as jnp
from jax import lax
from jax.experimental import pallas as pl
from jax.experimental.pallas import tpu as pltpu
from jax.sharding import PartitionSpec as P

MESH = pl.DeviceIdType.MESH
F32, BF16 = jnp.float32, jnp.bfloat16
CAP = 160
EDGE = 128
COLS = 96
PER = 3
PARTS = 4
UNROLL = 32
UNROLL_GO = {16: 5, 8: 7}
HALF = 64
LAST = PARTS - 1


def fused(
    slot_of, row_of, opens, last_of, values_hbm, grad_out, degrees, features, weight,
    out_features, out_weight,
    values, source0, source1, source2, source3, run, part, ring1, ring2, mid, ring3, ring4, last_sum, z_in, agg, scale, z_first,
    w_send, w_own, w_in, w_out, w_plane, w_line, w_full, w_sib,
    load_sem, first_send, first_recv, get_send, get_recv, ring_send, ring_recv, z_send, z_recv, sib_send, sib_recv,
    plane_send, plane_recv, line_send, line_recv,
):
    row, col = lax.axis_index("row"), lax.axis_index("col")
    core = lax.rem(row, 2)
    z_hi = row // 2
    x, z_lo, y = col // 8, lax.rem(col // 4, 2), lax.rem(col, 4)
    z = z_hi * 2 + z_lo
    plane = x * 4 + y

    def at(ix=x, iz=z, iy=y, icore=core):
        return ((iz // 2) * 2 + icore, (ix * 2 + lax.rem(iz, 2)) * 4 + iy)

    def plane_dev(p):
        return at(ix=p // 4, iy=lax.rem(p, 4))

    def line_dev(k):
        return at(iz=k)

    def remote(src, dst, ss, rs, to):
        return pltpu.make_async_remote_copy(
            src_ref=src, dst_ref=dst, send_sem=ss, recv_sem=rs, device_id=to, device_id_type=MESH
        )

    sibling = at(icore=1 - core)
    source = (source0, source1, source2, source3)

    load_v = pltpu.make_async_copy(values_hbm, values, load_sem)
    load_v.start()

    barrier = pltpu.get_barrier_semaphore()

    def greet_plane(i, carry):
        pl.semaphore_signal(barrier, inc=1, device_id=plane_dev(lax.rem(plane + i, 16)), device_id_type=MESH)
        return carry

    def greet_line(i, carry):
        pl.semaphore_signal(barrier, inc=1, device_id=line_dev(lax.rem(z + i, 8)), device_id_type=MESH)
        return carry

    lax.fori_loop(1, 16, greet_plane, 0)
    lax.fori_loop(1, 8, greet_line, 0)
    pl.semaphore_signal(barrier, inc=1, device_id=sibling, device_id_type=MESH)

    inv_root = lax.rsqrt(degrees[...].astype(F32))
    for p in range(PER):
        scale[p * 128:p * 128 + 128, :] = jnp.broadcast_to(inv_root[p:p + 1, :], (128, 128)).T
    for j in range(PARTS):
        for p in range(PER):
            got = grad_out[p * 128:p * 128 + 128, j * 128:j * 128 + 128].astype(F32)
            source[j][row * PER + p] = (got * scale[p * 128:p * 128 + 128, :]).astype(BF16)

    pl.semaphore_wait(barrier, 23)

    def gather(j):
        up, down, far = lax.rem(z_hi + 1, 4), lax.rem(z_hi + 3, 4), lax.rem(z_hi + 2, 4)
        dev = lambda h: (h * 2 + core, col)
        cut = 1 + j % 2

        def copy(k, zh, to, start=0, size=PER):
            ref = source[j].at[pl.ds((zh * 2 + core) * PER + start, size)]
            return remote(ref, ref, get_send.at[j, k], get_recv.at[j, k], to)

        own_up, own_down, own_sib = copy(0, z_hi, dev(up)), copy(1, z_hi, dev(down)), copy(2, z_hi, sibling)
        fwd_up = copy(3, down, dev(up), 0, cut)
        fwd_down = copy(4, up, dev(down), cut, PER - cut)
        sib_down, sib_up = copy(5, down, sibling), copy(6, up, sibling)
        sib_far = copy(7, far, sibling)

        def own():
            own_up.start()
            own_down.start()
            own_sib.start()

        def forward():
            own_up.wait_recv()
            fwd_up.start()
            own_down.wait_recv()
            fwd_down.start()
            sib_down.start()
            sib_up.start()

        def finish():
            fwd_up.wait_recv()
            fwd_down.wait_recv()
            sib_far.start()
            own_sib.wait_recv()
            sib_down.wait_recv()
            sib_up.wait_recv()
            sib_far.wait_recv()

        def drain():
            for c in (own_up, own_down, own_sib, fwd_up, fwd_down, sib_down, sib_up, sib_far):
                c.wait_send()

        return own, forward, finish, drain

    gathers = [gather(j) for j in range(PARTS)]

    def products(j):
        def slot(t, acc):
            prod = lax.dot_general(
                values[slot_of[t]], source[j][row_of[t]], (((0,), (0,)), ((), ())), preferred_element_type=F32
            )
            acc = jnp.where(opens[t] == 1, prod, acc + prod)
            run[t] = acc.astype(BF16)
            return acc

        lax.fori_loop(0, CAP, slot, jnp.zeros((EDGE, EDGE), F32), unroll=UNROLL)

        def place(b, carry):
            c, p = b // PER, lax.rem(b, PER)
            cx, cz, cy = c // 8, lax.rem(c // 4, 2), lax.rem(c, 4)
            end = last_of[b]
            got = run[jnp.maximum(end, 0)]
            got = jnp.where(end >= 0, got, jnp.zeros_like(got))
            for d, uv in ((0, cx * 4 + cy), (1, cy * 4 + cx)):
                i = (cz * 16 + uv if j == LAST else uv * 2 + cz) * PER + p
                part[j, d, i] = got[d * HALF:d * HALF + HALF]
            return carry

        lax.fori_loop(0, COLS, place, 0, unroll=4)

    def scaled_sum(j, d, p, total):
        rows = slice(p * 128 + d * HALF, p * 128 + d * HALF + HALF)
        agg[rows, j * 128:j * 128 + 128] = (total * scale[rows, :]).astype(BF16)

    def ring(j, side, stage):
        on_x = (side + stage) % 2 == 0
        u = x if on_x else y
        n = (24, 6)[stage] // (2 if j == LAST else 1)
        h = n // 2 + (side if n % 2 else 0)
        src = mid.at[j, side] if stage else z_first.at[side] if j == LAST else part.at[j, side]
        one = (ring1 if stage == 0 else ring3).at[j, side]
        two = (ring2 if stage == 0 else ring4).at[j, side]
        right, left, far = lax.rem(u + 1, 4), lax.rem(u + 3, 4), lax.rem(u + 2, 4)
        dev = (lambda k: at(ix=k)) if on_x else (lambda k: at(iy=k))

        def copy(k, a, b, to):
            return remote(a, b, ring_send.at[j, side, stage, k], ring_recv.at[j, side, stage, k], dev(to))

        c = [
            copy(0, src.at[pl.ds(far * n, h)], one.at[0, pl.ds(0, h)], right),
            copy(1, src.at[pl.ds(far * n + h, n - h)], one.at[1, pl.ds(0, n - h)], left),
            copy(2, src.at[pl.ds(right * n + h, n - h)], two.at[0, pl.ds(h, n - h)], right),
            copy(3, src.at[pl.ds(left * n, h)], two.at[1, pl.ds(0, h)], left),
            copy(4, one.at[0, pl.ds(0, h)], two.at[0, pl.ds(0, h)], right),
            copy(5, one.at[1, pl.ds(0, n - h)], two.at[1, pl.ds(h, n - h)], left),
        ]

        def second(k):
            base, count = ((right * n, h), (left * n + h, n - h))[k]
            wide = 3 if count % 3 == 0 else count
            c[k].wait_recv()

            def add(i, carry):
                at3, from3 = pl.ds(i * wide, wide), pl.ds(base + i * wide, wide)
                one[k, at3] = (one[k, at3].astype(F32) + src[from3].astype(F32)).astype(BF16)
                return carry

            lax.fori_loop(0, count // wide, add, 0)
            c[4 + k].start()

        def third():
            for k in range(2, 6):
                c[k].wait_recv()

            def add(i, carry):
                at3 = pl.ds(i * 3, 3)
                v = src[pl.ds(u * n + i * 3, 3)].astype(F32) + two[0, at3].astype(F32) + two[1, at3].astype(F32)
                if stage == 0:
                    mid[j, side, at3] = v.astype(BF16)
                elif j == LAST:
                    for p in range(PER):
                        scaled_sum(j, side, p, v[p])
                else:
                    last_sum[j, i, side] = v.astype(BF16)
                return carry

            lax.fori_loop(0, n // 3, add, 0)

        return c, second, third

    rings = {(j, d, s): ring(j, d, s) for j in range(PARTS) for d in (0, 1) for s in (0, 1)}
    z_copy = [
        remote(last_sum.at[j, 1 - z_lo], z_in.at[j], z_send.at[j], z_recv.at[j], at(iz=z_hi * 2 + 1 - z_lo))
        for j in range(LAST)
    ]

    def swap(d, k):
        u = lax.rem((x, y)[d] + k, 4)
        cut = pl.ds(u * 12, 12)
        c = remote(
            part.at[LAST, d, pl.ds((1 - z_lo) * 48 + u * 12, 12)], z_first.at[d, cut], first_send.at[d, k],
            first_recv.at[d, k], at(iz=z_hi * 2 + 1 - z_lo),
        )

        def take():
            c.wait_recv()

            def add(i, carry):
                at3 = pl.ds(u * 12 + i * 3, 3)
                own_part = part[LAST, d, pl.ds(z_lo * 48 + u * 12 + i * 3, 3)]
                z_first[d, at3] = (z_first[d, at3].astype(F32) + own_part.astype(F32)).astype(BF16)
                return carry

            lax.fori_loop(0, 4, add, 0)

        return c, take

    swaps = {(d, k): swap(d, k) for d in (0, 1) for k in range(4)}

    def give_z(k):
        for d in (0, 1):
            swaps[d, k][0].start()

    def take_z(k):
        for d in (0, 1):
            swaps[d, k][1]()

    def r1(j, which=(0, 1, 2, 3), stage=0):
        for k in which:
            for d in (0, 1):
                rings[j, d, stage][0][k].start()

    def r2(j, stage=0):
        for k in (0, 1):
            for d in (0, 1):
                rings[j, d, stage][1](k)

    def r3(j):
        for d in (0, 1):
            rings[j, d, 0][2]()
            for k in range(4):
                rings[j, d, 1][0][k].start()

    def r4(j):
        r2(j, 1)

    def r5(j):
        for d in (0, 1):
            rings[j, d, 1][2]()
        if j < LAST:
            z_copy[j].start()

    def r6(j):
        z_copy[j].wait_recv()
        for p in range(PER):
            for d in (0, 1):
                scaled_sum(j, d, p, last_sum[j, z_lo, d, p].astype(F32) + z_in[j, d, p].astype(F32))

    def exchange(count, me, dev, src_of, dst, ss, rs):
        def go(i, carry):
            to = lax.rem(me + i, count)
            remote(src_of(to), dst.at[me], ss, rs, dev(to)).start()
            return carry

        whole = remote(dst.at[pl.ds(0, count - 1)], dst.at[pl.ds(0, count - 1)], ss, rs, dev(lax.rem(me + 1, count)))
        return lambda: lax.fori_loop(1, count, go, 0, unroll=UNROLL_GO[count]), whole.wait_recv, whole.wait_send

    def weight_sum(g):
        give = remote(w_send.at[g], w_in.at[g], sib_send.at[g, 0], sib_recv.at[g, 0], sibling)
        back = remote(w_full.at[g], w_sib.at[g], sib_send.at[g, 1], sib_recv.at[g, 1], sibling)
        go1, arrive1, drain1 = exchange(
            16, plane, plane_dev, lambda to: w_out.at[g, to], w_plane.at[g], plane_send.at[g, 0], plane_recv.at[g, 0])
        go2, arrive2, drain2 = exchange(
            8, z, line_dev, lambda to: w_line.at[g, z], w_line.at[g], line_send.at[g], line_recv.at[g])
        go3, arrive3, drain3 = exchange(
            16, plane, plane_dev, lambda to: w_full.at[g, plane], w_full.at[g], plane_send.at[g, 1], plane_recv.at[g, 1])

        def half(which, dst):
            f = features[:, pl.ds(pl.multiple_of(which * 256, 256), 256)]
            for k in range(2):
                lanes = slice((g * 2 + k) * 128, (g * 2 + k) * 128 + 128)
                d = lax.dot_general(f, agg[:, lanes], (((0,), (0,)), ((), ())), preferred_element_type=F32)
                for q in range(8):
                    dst[g, k * 8 + q] = d[q * 32:q * 32 + 32, :].astype(dst.dtype)

        def a():
            half(1 - core, w_send)
            give.start()
            half(core, w_own)

        def b():
            give.wait_recv()
            for p in range(16):
                w_out[g, p] = (w_own[g, p] + w_in[g, p].astype(F32)).astype(BF16)
            go1()
            w_plane[g, plane] = w_out[g, plane]

        def c():
            arrive1()
            total = w_plane[g, 0].astype(F32)
            for p in range(1, 16):
                total = total + w_plane[g, p].astype(F32)
            w_line[g, z] = total.astype(BF16)
            go2()

        def d():
            arrive2()
            total = w_line[g, 0].astype(F32)
            for k in range(1, 8):
                total = total + w_line[g, k].astype(F32)
            w_full[g, plane] = total.astype(BF16)
            go3()

        def write(which, src):
            base = pl.multiple_of(which * 256, 256)
            for k in range(2):
                for q in range(8):
                    out_weight[pl.ds(base + q * 32, 32), (g * 2 + k) * 128:(g * 2 + k) * 128 + 128] = (
                        src[g, k * 8 + q].astype(F32)
                    )

        def e():
            arrive3()
            back.start()
            write(core, w_full)

        def f():
            back.wait_recv()
            write(1 - core, w_sib)

        def drain():
            give.wait_send()
            back.wait_send()
            drain1()
            drain2()
            drain3()

        return a, b, c, d, e, f, drain

    ws = [weight_sum(g) for g in range(2)]

    own, forward, finish = [[g[i] for g in gathers] for i in range(3)]
    own[0]()
    own[1]()
    forward[0]()
    own[2]()
    forward[1]()
    own[3]()
    finish[0]()
    load_v.wait()
    products(0)
    r1(0)
    forward[2]()
    finish[1]()
    products(1)
    r2(0)
    r1(1)
    forward[3]()
    finish[2]()
    products(2)
    r3(0)
    finish[3]()
    products(3)
    give_z(2)
    give_z(1)
    give_z(3)
    r2(1)
    r1(2)
    r4(0)
    r5(0)
    r3(1)
    take_z(2)
    r1(3, (0, 1))
    r2(2)
    take_z(1)
    r1(3, (2,))
    r4(1)
    r5(1)
    give_z(0)
    r3(2)
    take_z(3)
    r1(3, (3,))
    r2(3)
    r6(0)
    r6(1)
    ws[0][0]()
    r4(2)
    ws[0][1]()
    r5(2)
    take_z(0)
    r3(3)
    ws[0][2]()
    r4(3)
    r6(2)
    ws[0][3]()
    r5(3)
    ws[1][0]()
    ws[1][1]()
    ws[0][4]()
    out_features[...] = lax.dot_general(
        agg[...], weight[...], (((1,), (1,)), ((), ())), preferred_element_type=F32
    ).astype(BF16)
    for j in range(PARTS):
        gathers[j][3]()
    for c in z_copy:
        c.wait_send()
    for key in swaps:
        swaps[key][0].wait_send()
    for key in rings:
        for c in rings[key][0]:
            c.wait_send()
    ws[0][5]()
    ws[1][2]()
    ws[0][6]()
    ws[1][3]()
    ws[1][4]()
    ws[1][5]()
    ws[1][6]()


def slot_table(coords, count):
    index = jnp.arange(CAP, dtype=jnp.int32)
    live = index < count
    rows, cols = coords[:, 0], coords[:, 1]
    key = jnp.where(live, cols * 32 + rows, 4096 + index)
    rank = jnp.sum((key[None, :] < key[:, None]).astype(jnp.int32), axis=1)
    hit = rank[None, :] == index[:, None]
    pick = lambda v: jnp.sum(jnp.where(hit, v[None, :], 0), axis=1)
    first = jnp.ones((CAP,), jnp.int32)
    order, srow, scol = pick(index), pick(rows), pick(cols)
    first = jnp.concatenate([first[:1], (scol[1:] != scol[:-1]).astype(jnp.int32)])
    lanes = jnp.arange(COLS, dtype=jnp.int32)[:, None]
    upto = jnp.sum((live & (cols <= lanes)).astype(jnp.int32), axis=1)
    has = jnp.any(live & (cols == lanes), axis=1)
    end = jnp.where(has, upto - 1, -1)
    return order, srow, first, end


def body(grad_out, features, weight, degrees, block_coords, block_values, block_counts):
    table = slot_table(block_coords[0, 0], block_counts[0, 0])
    vm = lambda *s: pltpu.VMEM(s, BF16)
    vf = lambda *s: pltpu.VMEM(s, F32)
    dma = lambda *s: pltpu.SemaphoreType.DMA(s)
    any_spec, vmem_spec = pl.BlockSpec(memory_space=pl.ANY), pl.BlockSpec(memory_space=pltpu.VMEM)
    return pl.pallas_call(
        fused,
        out_shape=(jax.ShapeDtypeStruct((384, 512), BF16), jax.ShapeDtypeStruct((512, 512), F32)),
        in_specs=[pl.BlockSpec(memory_space=pltpu.SMEM)] * 4 + [any_spec, vmem_spec, vmem_spec, vmem_spec, vmem_spec],
        out_specs=(vmem_spec, vmem_spec),
        scratch_shapes=[
            vm(CAP, EDGE, EDGE), vm(24, EDGE, EDGE), vm(24, EDGE, EDGE), vm(24, EDGE, EDGE), vm(24, EDGE, EDGE), vm(CAP, EDGE, EDGE), vm(PARTS, 2, COLS, HALF, EDGE),
            vm(PARTS, 2, 2, 12, HALF, EDGE), vm(PARTS, 2, 2, 24, HALF, EDGE), vm(PARTS, 2, 24, HALF, EDGE),
            vm(PARTS, 2, 2, 3, HALF, EDGE), vm(PARTS, 2, 2, 6, HALF, EDGE), vm(PARTS, 2, 2, PER, HALF, EDGE),
            vm(PARTS, 2, PER, HALF, EDGE), vm(384, 512), vf(384, 128), vm(2, 48, HALF, EDGE),
            vm(2, 16, 32, 128), vf(2, 16, 32, 128), vm(2, 16, 32, 128), vm(2, 16, 32, 128), vm(2, 16, 32, 128),
            vm(2, 8, 32, 128), vm(2, 16, 32, 128), vm(2, 16, 32, 128),
            pltpu.SemaphoreType.DMA, dma(2, 4), dma(2, 4), dma(PARTS, 8), dma(PARTS, 8), dma(PARTS, 2, 2, 6), dma(PARTS, 2, 2, 6),
            dma(PARTS), dma(PARTS), dma(2, 2), dma(2, 2),
            dma(2, 2), dma(2, 2), dma(2), dma(2),
        ],
        compiler_params=pltpu.CompilerParams(
            collective_id=0, has_side_effects=True, vmem_limit_bytes=60 * 1024 * 1024
        ),
    )(*table, block_values[0, 0], grad_out, degrees.reshape(PER, 128), features, weight)


def solution(mesh):
    in_specs = (
        P(("row", "col"), None),
        P(("row", "col"), None),
        P(),
        P(("row", "col")),
        P("row", "col", None, None),
        P("row", "col", None, None, None),
        P("row", "col"),
    )
    out_specs = (P(("row", "col"), None), P())
    return jax.shard_map(body, mesh=mesh, in_specs=in_specs, out_specs=out_specs, check_vma=False)
```

```python
import functools

import jax
import jax.numpy as jnp
from jax import lax
from jax.experimental import pallas as pl
from jax.experimental.pallas import tpu as pltpu
from jax.sharding import PartitionSpec as P

MESH = pl.DeviceIdType.MESH
F32, BF16 = jnp.float32, jnp.bfloat16
CAP = 160
EDGE = 128
COLS = 96
PER = 3
PARTS = 4
UNROLL = 32
UNROLL_GO = {16: 5, 8: 7}
HALF = 64
LAST = PARTS - 1


def fused(
    slot_of, row_of, opens, last_of, values_hbm, grad_out, degrees, features, weight,
    out_features, out_weight,
    values, source0, source1, source2, source3, run, part, ring1, ring2, mid, ring3, ring4, last_sum, z_in, agg, scale, z_first,
    w_send, w_own, w_in, w_out, w_plane, w_line, w_full, w_sib,
    load_sem, first_send, first_recv, get_send, get_recv, ring_send, ring_recv, z_send, z_recv, sib_send, sib_recv,
    plane_send, plane_recv, line_send, line_recv,
):
    row, col = lax.axis_index("row"), lax.axis_index("col")
    core = lax.rem(row, 2)
    z_hi = row // 2
    x, z_lo, y = col // 8, lax.rem(col // 4, 2), lax.rem(col, 4)
    z = z_hi * 2 + z_lo
    plane = x * 4 + y

    def at(ix=x, iz=z, iy=y, icore=core):
        return ((iz // 2) * 2 + icore, (ix * 2 + lax.rem(iz, 2)) * 4 + iy)

    def plane_dev(p):
        return at(ix=p // 4, iy=lax.rem(p, 4))

    def line_dev(k):
        return at(iz=k)

    def remote(src, dst, ss, rs, to):
        return pltpu.make_async_remote_copy(
            src_ref=src, dst_ref=dst, send_sem=ss, recv_sem=rs, device_id=to, device_id_type=MESH
        )

    sibling = at(icore=1 - core)
    source = (source0, source1, source2, source3)

    load_v = pltpu.make_async_copy(values_hbm, values, load_sem)
    load_v.start()

    barrier = pltpu.get_barrier_semaphore()

    def greet_plane(i, carry):
        pl.semaphore_signal(barrier, inc=1, device_id=plane_dev(lax.rem(plane + i, 16)), device_id_type=MESH)
        return carry

    def greet_line(i, carry):
        pl.semaphore_signal(barrier, inc=1, device_id=line_dev(lax.rem(z + i, 8)), device_id_type=MESH)
        return carry

    lax.fori_loop(1, 16, greet_plane, 0)
    lax.fori_loop(1, 8, greet_line, 0)
    pl.semaphore_signal(barrier, inc=1, device_id=sibling, device_id_type=MESH)

    inv_root = lax.rsqrt(degrees[...].astype(F32))
    for p in range(PER):
        scale[p * 128:p * 128 + 128, :] = jnp.broadcast_to(inv_root[p:p + 1, :], (128, 128)).T
    for j in range(PARTS):
        for p in range(PER):
            got = grad_out[p * 128:p * 128 + 128, j * 128:j * 128 + 128].astype(F32)
            source[j][row * PER + p] = (got * scale[p * 128:p * 128 + 128, :]).astype(BF16)

    pl.semaphore_wait(barrier, 23)

    def gather(j):
        up, down, far = lax.rem(z_hi + 1, 4), lax.rem(z_hi + 3, 4), lax.rem(z_hi + 2, 4)
        dev = lambda h: (h * 2 + core, col)
        cut = 1 + j % 2

        def copy(k, zh, to, start=0, size=PER):
            ref = source[j].at[pl.ds((zh * 2 + core) * PER + start, size)]
            return remote(ref, ref, get_send.at[j, k], get_recv.at[j, k], to)

        own_up, own_down, own_sib = copy(0, z_hi, dev(up)), copy(1, z_hi, dev(down)), copy(2, z_hi, sibling)
        fwd_up = copy(3, down, dev(up), 0, cut)
        fwd_down = copy(4, up, dev(down), cut, PER - cut)
        sib_down, sib_up = copy(5, down, sibling), copy(6, up, sibling)
        sib_far = copy(7, far, sibling)

        def own():
            own_up.start()
            own_down.start()
            own_sib.start()

        def forward():
            own_up.wait_recv()
            fwd_up.start()
            own_down.wait_recv()
            fwd_down.start()
            sib_down.start()
            sib_up.start()

        def finish():
            fwd_up.wait_recv()
            fwd_down.wait_recv()
            sib_far.start()
            own_sib.wait_recv()
            sib_down.wait_recv()
            sib_up.wait_recv()
            sib_far.wait_recv()

        def drain():
            for c in (own_up, own_down, own_sib, fwd_up, fwd_down, sib_down, sib_up, sib_far):
                c.wait_send()

        return own, forward, finish, drain

    gathers = [gather(j) for j in range(PARTS)]

    def products(j):
        def slot(t, acc):
            prod = lax.dot_general(
                values[slot_of[t]], source[j][row_of[t]], (((0,), (0,)), ((), ())), preferred_element_type=F32
            )
            acc = jnp.where(opens[t] == 1, prod, acc + prod)
            run[t] = acc.astype(BF16)
            return acc

        lax.fori_loop(0, CAP, slot, jnp.zeros((EDGE, EDGE), F32), unroll=UNROLL)

        def place(b, carry):
            c, p = b // PER, lax.rem(b, PER)
            cx, cz, cy = c // 8, lax.rem(c // 4, 2), lax.rem(c, 4)
            end = last_of[b]
            got = run[jnp.maximum(end, 0)]
            got = jnp.where(end >= 0, got, jnp.zeros_like(got))
            for d, uv in ((0, cx * 4 + cy), (1, cy * 4 + cx)):
                i = (cz * 16 + uv if j == LAST else uv * 2 + cz) * PER + p
                part[j, d, i] = got[d * HALF:d * HALF + HALF]
            return carry

        lax.fori_loop(0, COLS, place, 0, unroll=4)

    def scaled_sum(j, d, p, total):
        rows = slice(p * 128 + d * HALF, p * 128 + d * HALF + HALF)
        agg[rows, j * 128:j * 128 + 128] = (total * scale[rows, :]).astype(BF16)

    def ring(j, side, stage):
        on_x = (side + stage) % 2 == 0
        u = x if on_x else y
        n = (24, 6)[stage] // (2 if j == LAST else 1)
        h = n // 2 + (side if n % 2 else 0)
        src = mid.at[j, side] if stage else z_first.at[side] if j == LAST else part.at[j, side]
        one = (ring1 if stage == 0 else ring3).at[j, side]
        two = (ring2 if stage == 0 else ring4).at[j, side]
        right, left, far = lax.rem(u + 1, 4), lax.rem(u + 3, 4), lax.rem(u + 2, 4)
        dev = (lambda k: at(ix=k)) if on_x else (lambda k: at(iy=k))

        def copy(k, a, b, to):
            return remote(a, b, ring_send.at[j, side, stage, k], ring_recv.at[j, side, stage, k], dev(to))

        c = [
            copy(0, src.at[pl.ds(far * n, h)], one.at[0, pl.ds(0, h)], right),
            copy(1, src.at[pl.ds(far * n + h, n - h)], one.at[1, pl.ds(0, n - h)], left),
            copy(2, src.at[pl.ds(right * n + h, n - h)], two.at[0, pl.ds(h, n - h)], right),
            copy(3, src.at[pl.ds(left * n, h)], two.at[1, pl.ds(0, h)], left),
            copy(4, one.at[0, pl.ds(0, h)], two.at[0, pl.ds(0, h)], right),
            copy(5, one.at[1, pl.ds(0, n - h)], two.at[1, pl.ds(h, n - h)], left),
        ]

        def second(k):
            base, count = ((right * n, h), (left * n + h, n - h))[k]
            wide = 3 if count % 3 == 0 else count
            c[k].wait_recv()

            def add(i, carry):
                at3, from3 = pl.ds(i * wide, wide), pl.ds(base + i * wide, wide)
                one[k, at3] = (one[k, at3].astype(F32) + src[from3].astype(F32)).astype(BF16)
                return carry

            lax.fori_loop(0, count // wide, add, 0)
            c[4 + k].start()

        def third():
            for k in range(2, 6):
                c[k].wait_recv()

            def add(i, carry):
                at3 = pl.ds(i * 3, 3)
                v = src[pl.ds(u * n + i * 3, 3)].astype(F32) + two[0, at3].astype(F32) + two[1, at3].astype(F32)
                if stage == 0:
                    mid[j, side, at3] = v.astype(BF16)
                elif j == LAST:
                    for p in range(PER):
                        scaled_sum(j, side, p, v[p])
                else:
                    last_sum[j, i, side] = v.astype(BF16)
                return carry

            lax.fori_loop(0, n // 3, add, 0)

        return c, second, third

    rings = {(j, d, s): ring(j, d, s) for j in range(PARTS) for d in (0, 1) for s in (0, 1)}
    z_copy = [
        remote(last_sum.at[j, 1 - z_lo], z_in.at[j], z_send.at[j], z_recv.at[j], at(iz=z_hi * 2 + 1 - z_lo))
        for j in range(LAST)
    ]

    def swap(d, k):
        u = lax.rem((x, y)[d] + k, 4)
        cut = pl.ds(u * 12, 12)
        c = remote(
            part.at[LAST, d, pl.ds((1 - z_lo) * 48 + u * 12, 12)], z_first.at[d, cut], first_send.at[d, k],
            first_recv.at[d, k], at(iz=z_hi * 2 + 1 - z_lo),
        )

        def take():
            c.wait_recv()

            def add(i, carry):
                at3 = pl.ds(u * 12 + i * 3, 3)
                own_part = part[LAST, d, pl.ds(z_lo * 48 + u * 12 + i * 3, 3)]
                z_first[d, at3] = (z_first[d, at3].astype(F32) + own_part.astype(F32)).astype(BF16)
                return carry

            lax.fori_loop(0, 4, add, 0)

        return c, take

    swaps = {(d, k): swap(d, k) for d in (0, 1) for k in range(4)}

    def give_z(k):
        for d in (0, 1):
            swaps[d, k][0].start()

    def take_z(k):
        for d in (0, 1):
            swaps[d, k][1]()

    def r1(j, which=(0, 1, 2, 3), stage=0):
        for k in which:
            for d in (0, 1):
                rings[j, d, stage][0][k].start()

    def r2(j, stage=0):
        for k in (0, 1):
            for d in (0, 1):
                rings[j, d, stage][1](k)

    def r3(j):
        for d in (0, 1):
            rings[j, d, 0][2]()
            for k in range(4):
                rings[j, d, 1][0][k].start()

    def r4(j):
        r2(j, 1)

    def r5(j):
        for d in (0, 1):
            rings[j, d, 1][2]()
        if j < LAST:
            z_copy[j].start()

    def r6(j):
        z_copy[j].wait_recv()
        for p in range(PER):
            for d in (0, 1):
                scaled_sum(j, d, p, last_sum[j, z_lo, d, p].astype(F32) + z_in[j, d, p].astype(F32))

    def exchange(count, me, dev, src_of, dst, ss, rs):
        def go(i, carry):
            to = lax.rem(me + i, count)
            remote(src_of(to), dst.at[me], ss, rs, dev(to)).start()
            return carry

        whole = remote(dst.at[pl.ds(0, count - 1)], dst.at[pl.ds(0, count - 1)], ss, rs, dev(lax.rem(me + 1, count)))
        return lambda: lax.fori_loop(1, count, go, 0, unroll=UNROLL_GO[count]), whole.wait_recv, whole.wait_send

    def weight_sum(g):
        give = remote(w_send.at[g], w_in.at[g], sib_send.at[g, 0], sib_recv.at[g, 0], sibling)
        back = remote(w_full.at[g], w_sib.at[g], sib_send.at[g, 1], sib_recv.at[g, 1], sibling)
        go1, arrive1, drain1 = exchange(
            16, plane, plane_dev, lambda to: w_out.at[g, to], w_plane.at[g], plane_send.at[g, 0], plane_recv.at[g, 0])
        go2, arrive2, drain2 = exchange(
            8, z, line_dev, lambda to: w_line.at[g, z], w_line.at[g], line_send.at[g], line_recv.at[g])
        go3, arrive3, drain3 = exchange(
            16, plane, plane_dev, lambda to: w_full.at[g, plane], w_full.at[g], plane_send.at[g, 1], plane_recv.at[g, 1])

        def half(which, dst):
            f = features[:, pl.ds(pl.multiple_of(which * 256, 256), 256)]
            for k in range(2):
                lanes = slice((g * 2 + k) * 128, (g * 2 + k) * 128 + 128)
                d = lax.dot_general(f, agg[:, lanes], (((0,), (0,)), ((), ())), preferred_element_type=F32)
                for q in range(8):
                    dst[g, k * 8 + q] = d[q * 32:q * 32 + 32, :].astype(dst.dtype)

        def a():
            half(1 - core, w_send)
            give.start()
            half(core, w_own)

        def b():
            give.wait_recv()
            for p in range(16):
                w_out[g, p] = (w_own[g, p] + w_in[g, p].astype(F32)).astype(BF16)
            go1()
            w_plane[g, plane] = w_out[g, plane]

        def c():
            arrive1()
            total = w_plane[g, 0].astype(F32)
            for p in range(1, 16):
                total = total + w_plane[g, p].astype(F32)
            w_line[g, z] = total.astype(BF16)
            go2()

        def d():
            arrive2()
            total = w_line[g, 0].astype(F32)
            for k in range(1, 8):
                total = total + w_line[g, k].astype(F32)
            w_full[g, plane] = total.astype(BF16)
            go3()

        def write(which, src):
            base = pl.multiple_of(which * 256, 256)
            for k in range(2):
                for q in range(8):
                    out_weight[pl.ds(base + q * 32, 32), (g * 2 + k) * 128:(g * 2 + k) * 128 + 128] = (
                        src[g, k * 8 + q].astype(F32)
                    )

        def e():
            arrive3()
            back.start()
            write(core, w_full)

        def f():
            back.wait_recv()
            write(1 - core, w_sib)

        def drain():
            give.wait_send()
            back.wait_send()
            drain1()
            drain2()
            drain3()

        return a, b, c, d, e, f, drain

    ws = [weight_sum(g) for g in range(2)]

    own, forward, finish = [[g[i] for g in gathers] for i in range(3)]
    own[0]()
    own[1]()
    forward[0]()
    own[2]()
    forward[1]()
    own[3]()
    finish[0]()
    load_v.wait()
    products(0)
    r1(0)
    forward[2]()
    finish[1]()
    products(1)
    r2(0)
    r1(1)
    forward[3]()
    finish[2]()
    products(2)
    r3(0)
    finish[3]()
    products(3)
    give_z(2)
    give_z(1)
    give_z(3)
    r2(1)
    r1(2)
    r4(0)
    r5(0)
    r3(1)
    take_z(2)
    r1(3, (0, 1))
    r2(2)
    take_z(1)
    r1(3, (2,))
    r4(1)
    r5(1)
    give_z(0)
    r3(2)
    take_z(3)
    r1(3, (3,))
    r2(3)
    r6(0)
    r6(1)
    ws[0][0]()
    r4(2)
    ws[0][1]()
    r5(2)
    take_z(0)
    r3(3)
    ws[0][2]()
    r4(3)
    r6(2)
    ws[0][3]()
    r5(3)
    ws[1][0]()
    ws[1][1]()
    ws[0][4]()
    out_features[...] = lax.dot_general(
        agg[...], weight[...], (((1,), (1,)), ((), ())), preferred_element_type=F32
    ).astype(BF16)
    for j in range(PARTS):
        gathers[j][3]()
    for c in z_copy:
        c.wait_send()
    for key in swaps:
        swaps[key][0].wait_send()
    for key in rings:
        for c in rings[key][0]:
            c.wait_send()
    ws[0][5]()
    ws[1][2]()
    ws[0][6]()
    ws[1][3]()
    ws[1][4]()
    ws[1][5]()
    ws[1][6]()


def ship(features, weight, out_features, out_weight):
    out_weight[...] = weight[...]
    out_features[...] = features[...]


def slot_table(coords, count):
    index = jnp.arange(CAP, dtype=jnp.int32)
    live = index < count
    rows, cols = coords[:, 0], coords[:, 1]
    key = jnp.where(live, cols * 32 + rows, 4096 + index)
    rank = jnp.sum((key[None, :] < key[:, None]).astype(jnp.int32), axis=1)
    hit = rank[None, :] == index[:, None]
    pick = lambda v: jnp.sum(jnp.where(hit, v[None, :], 0), axis=1)
    first = jnp.ones((CAP,), jnp.int32)
    order, srow, scol = pick(index), pick(rows), pick(cols)
    first = jnp.concatenate([first[:1], (scol[1:] != scol[:-1]).astype(jnp.int32)])
    lanes = jnp.arange(COLS, dtype=jnp.int32)[:, None]
    upto = jnp.sum((live & (cols <= lanes)).astype(jnp.int32), axis=1)
    has = jnp.any(live & (cols == lanes), axis=1)
    end = jnp.where(has, upto - 1, -1)
    return order, srow, first, end


def body(grad_out, features, weight, degrees, block_coords, block_values, block_counts):
    table = slot_table(block_coords[0, 0], block_counts[0, 0])
    vm = lambda *s: pltpu.VMEM(s, BF16)
    vf = lambda *s: pltpu.VMEM(s, F32)
    dma = lambda *s: pltpu.SemaphoreType.DMA(s)
    any_spec, vmem_spec = pl.BlockSpec(memory_space=pl.ANY), pl.BlockSpec(memory_space=pltpu.VMEM)
    shapes = (jax.ShapeDtypeStruct((384, 512), BF16), jax.ShapeDtypeStruct((512, 512), F32))
    results = pl.pallas_call(
        fused,
        out_shape=shapes,
        in_specs=[pl.BlockSpec(memory_space=pltpu.SMEM)] * 4 + [any_spec, vmem_spec, vmem_spec, vmem_spec, vmem_spec],
        out_specs=(vmem_spec, vmem_spec),
        scratch_shapes=[
            vm(CAP, EDGE, EDGE), vm(24, EDGE, EDGE), vm(24, EDGE, EDGE), vm(24, EDGE, EDGE), vm(24, EDGE, EDGE), vm(CAP, EDGE, EDGE), vm(PARTS, 2, COLS, HALF, EDGE),
            vm(PARTS, 2, 2, 12, HALF, EDGE), vm(PARTS, 2, 2, 24, HALF, EDGE), vm(PARTS, 2, 24, HALF, EDGE),
            vm(PARTS, 2, 2, 3, HALF, EDGE), vm(PARTS, 2, 2, 6, HALF, EDGE), vm(PARTS, 2, 2, PER, HALF, EDGE),
            vm(PARTS, 2, PER, HALF, EDGE), vm(384, 512), vf(384, 128), vm(2, 48, HALF, EDGE),
            vm(2, 16, 32, 128), vf(2, 16, 32, 128), vm(2, 16, 32, 128), vm(2, 16, 32, 128), vm(2, 16, 32, 128),
            vm(2, 8, 32, 128), vm(2, 16, 32, 128), vm(2, 16, 32, 128),
            pltpu.SemaphoreType.DMA, dma(2, 4), dma(2, 4), dma(PARTS, 8), dma(PARTS, 8), dma(PARTS, 2, 2, 6), dma(PARTS, 2, 2, 6),
            dma(PARTS), dma(PARTS), dma(2, 2), dma(2, 2),
            dma(2, 2), dma(2, 2), dma(2), dma(2),
        ],
        compiler_params=pltpu.CompilerParams(
            collective_id=0, has_side_effects=True, vmem_limit_bytes=60 * 1024 * 1024
        ),
    )(*table, block_values[0, 0], grad_out, degrees.reshape(PER, 128), features, weight)
    return pl.pallas_call(
        ship,
        out_shape=shapes,
        in_specs=[vmem_spec, vmem_spec],
        out_specs=(vmem_spec, vmem_spec),
    )(*results)


def solution(mesh):
    in_specs = (
        P(("row", "col"), None),
        P(("row", "col"), None),
        P(),
        P(("row", "col")),
        P("row", "col", None, None),
        P("row", "col", None, None, None),
        P("row", "col"),
    )
    out_specs = (P(("row", "col"), None), P())
    return jax.shard_map(body, mesh=mesh, in_specs=in_specs, out_specs=out_specs, check_vma=False)
```
